256 devices in a mesh: occ: 64 (over x_hi, z, y), aux: 4 (over x_lo, core).
Axes of the slice: x: 4 (x_hi: 2, x_lo: 2; x = x_hi * 2 + x_lo), y: 4, z: 8, core: 2. Of those that a mesh axis runs over, the one named last changes fastest.
Arguments:
- b_tensor: bfloat16 [24000, 256, 128], P('aux', 'occ'), may hold values from -1.25 to 1.25
- occ_energy: float32 [256], replicated, may hold values from -1.5 to -0.3
- vir_energy: float32 [128], replicated, may hold values from 0.3 to 3
- occ_count: int32 [64], replicated, may hold values from 1 to 4, 192 in all
Outputs:
- gamma: bfloat16 [24000, 256, 128], P('aux', 'occ')
The draws below stay inside these ranges and needn't reach their ends.
Inputs may be any that keep to these rules, and one draw needn't show every extreme that they name: `occ_count`: each block has at least one live orbital; some block has all 4 live.
All inputs are finite; a program needn't handle non-finite values.
Results may differ from the reference program's by a relative error of at most 0.0048.
Values may be sent and summed in bfloat16 or wider, within the bound.
A program may use at most 128 MiB of HBM per device.

```python
import math
import jax
import jax.numpy as jnp
import numpy as np
from jax import lax

NAUX = 24000
VPAN = 128
OCC_DEV = 4
NOCC = 256
N_OCC = 64


def level_of(own_key, dims, pieces, least, largest):
    def one(axis_at, shards_of):
        heights = jax.random.uniform(jax.random.fold_in(jax.random.fold_in(own_key, 6), axis_at), (shards_of,), jnp.float32, least / len(pieces), largest / len(pieces))
        return jnp.repeat(jnp.exp(heights), dims[axis_at] // shards_of).reshape((-1,) + (1,) * (len(dims) - axis_at - 1))

    level = one(*pieces[0])
    for cut in pieces[1:]:
        level = level * one(*cut)
    return level


def length_profile(count, total, limit, slope):
    loads = [(1 << 20) // math.isqrt(grade ** slope) + 1 for grade in range(2, count + 1)]
    rest, given = total - limit - (count - 1), [1] * (count - 1)
    while rest > 0:
        free = [i for i in range(count - 1) if given[i] < limit]
        whole, remaining = sum([loads[i] for i in free]), rest
        for i in free:
            more = min(limit - given[i], max(1, remaining * loads[i] // whole), rest)
            given[i] = given[i] + more
            rest = rest - more
    return np.array([limit] + given)


def ragged_sizes(rng, count, total, reach, lean):
    if count == 2:
        one = jax.random.randint(rng, (), max(1, total - reach), min(reach, total - 1) + 1)
        return jnp.stack([one, total - one])
    sizes = jnp.asarray(length_profile(count, total, reach, lean), jnp.int32)
    pairs = (count - 1) // 2
    giver, taker = sizes[1:1 + 2 * pairs:2], sizes[2:2 + 2 * pairs:2]
    margin = jnp.minimum(giver - 1, reach - taker)
    moved = jax.random.randint(jax.random.fold_in(rng, 1), (pairs,), 0, 1 << 20) % (margin + 1)
    sizes = sizes.at[1:1 + 2 * pairs:2].set(giver - moved).at[2:2 + 2 * pairs:2].set(taker + moved)
    return sizes[jax.random.permutation(jax.random.fold_in(rng, 2), count)]


def bell_draw(rng, shape, spread, most, shards=(), kind=jnp.bfloat16):
    gain = level_of(rng, shape, shards, -0.22, 0.18) if shards else 1.0
    entries = jax.random.normal(rng, shape, jnp.float32) * spread * gain
    return jnp.minimum(jnp.maximum(entries, -most), most).astype(kind)


def setup_inputs(seed: int = 0) -> dict:
    keys = jax.random.split(jax.random.key(seed), 5)
    return {
        "b_tensor": bell_draw(keys[0], (NAUX, NOCC, VPAN), (NAUX ** -0.25), 1.25, ((0, 4), (1, 64))),
        "occ_energy": jnp.clip(jax.random.uniform(keys[1], (NOCC,), jnp.float32, -1.5, -0.3), -1.5, -0.3),
        "vir_energy": jnp.clip(jax.random.uniform(keys[2], (VPAN,), jnp.float32, 0.3, 3.0), 0.3, 3.0),
        "occ_count": ragged_sizes(keys[3], N_OCC, N_OCC * OCC_DEV * 3 // 4, OCC_DEV, 0).astype(jnp.int32),
    }


def amplitudes(kmat, occ_rows, occ_cols, vir, live_rows, live_cols):
    pair_energy = (occ_rows[:, None] + occ_cols[None, :]).reshape(-1)
    pair_live = (live_rows[:, None] * live_cols[None, :]).reshape(-1)
    flat = kmat.reshape(-1, kmat.shape[2], kmat.shape[3])
    denom = pair_energy[:, None, None] - vir[None, :, None] - vir[None, None, :]
    ampl = flat / denom
    twice = 2.0 * ampl - jnp.swapaxes(ampl, 1, 2)
    return (twice * pair_live[:, None, None]).astype(jnp.bfloat16).reshape(kmat.shape)


def reference(b_tensor, occ_energy, vir_energy, occ_count):
    blocks = b_tensor.reshape(NAUX, N_OCC, OCC_DEV, VPAN)
    energy = occ_energy.reshape(N_OCC, OCC_DEV)
    live = (jnp.arange(OCC_DEV, dtype=jnp.int32)[None, :] < occ_count[:, None]).astype(jnp.float32)
    half = N_OCC // 2

    def one_block(blk):
        mate = ((blk + half) % N_OCC).astype(jnp.int32)
        own = lax.dynamic_index_in_dim(blocks, blk, 1, keepdims=False).astype(jnp.float32)
        other = lax.dynamic_index_in_dim(blocks, mate, 1, keepdims=False).astype(jnp.float32)
        e_own = lax.dynamic_index_in_dim(energy, blk, 0, keepdims=False)
        e_other = lax.dynamic_index_in_dim(energy, mate, 0, keepdims=False)
        l_own = lax.dynamic_index_in_dim(live, blk, 0, keepdims=False)
        l_other = lax.dynamic_index_in_dim(live, mate, 0, keepdims=False)
        k_diag = jnp.einsum("pia,pjb->ijab", own, own)
        k_cross = jnp.einsum("pia,pjb->ijab", own, other)
        t_diag = amplitudes(k_diag, e_own, e_own, vir_energy, l_own, l_own)
        t_cross = amplitudes(k_cross, e_own, e_other, vir_energy, l_own, l_other)
        total = jnp.einsum("pjb,ijab->pia", own, t_diag.astype(jnp.float32))
        total = total + jnp.einsum("pjb,ijab->pia", other, t_cross.astype(jnp.float32))
        return total.astype(jnp.bfloat16)

    out = lax.map(one_block, jnp.arange(N_OCC, dtype=jnp.int32))
    return jnp.transpose(out, (1, 0, 2, 3)).reshape(NAUX, NOCC, VPAN)
```

```python
import functools

import jax
import jax.numpy as jnp
from jax import lax
from jax.experimental import pallas as pl
from jax.experimental.pallas import tpu as pltpu
from jax.sharding import PartitionSpec as P

CHUNKS = 9
AHEAD = 2
MESH = pl.DeviceIdType.MESH
F32, BF16 = jnp.float32, jnp.bfloat16
KSEND = jnp.float32


def kernel(dims, occ_energy, occ_count, vir, b, out, raw, wide, own, met, far, res, kd, kx, kd_rc, kx_rc,
           kd_out, kd_ri, kx_out, kx_rq, td, tx, tq, blk, load_sem, hop1_s, hop1_r, hop2_s, hop2_r, out_sem,
           ks, kr):
    n_occ, rows, nv, slots = dims
    flat = slots * nv
    half = rows // 2
    size = met.shape[1] // CHUNKS
    start1 = rows - size * CHUNKS
    over = size * CHUNKS - start1
    hv = flat // 2
    o, u = lax.axis_index("occ"), lax.axis_index("aux")
    blocks = n_occ // 2
    h, col = o // blocks, o % blocks
    lo, s = u // 2, u % 2
    x = 2 * h + lo
    u_in = (u + 2) % 4
    other = (o + blocks) % n_occ
    core = (o, u + 1 - 2 * s)
    inner, outer, diag = (o, u_in), (other, u_in), (other, u)

    barrier = pltpu.get_barrier_semaphore()
    for dev in ((o, u_in), (other, u_in), (other, u), core):
        pl.semaphore_signal(barrier, inc=1, device_id=dev, device_id_type=MESH)

    def load(q, c):
        at = slots * (q * start1 + c * size)
        return pltpu.make_async_copy(b.at[pl.ds(at, slots * size)], raw.at[q, c], load_sem.at[q, c])

    for c in range(CHUNKS):
        for q in range(2):
            load(q, c).start()

    def remote(src, dst, ss, rs, dev):
        return pltpu.make_async_remote_copy(src_ref=src, dst_ref=dst, send_sem=ss, recv_sem=rs, device_id=dev,
                                            device_id_type=MESH)

    def at(c):
        return pl.ds(pl.multiple_of(c * size, 16), size)

    def hop1(q, c):
        return remote(own.at[q, at(c)], met.at[h, at(c)], hop1_s.at[q, c], hop1_r.at[h, c],
                      (col + blocks * q, u_in))

    def hop2(t, c):
        return remote(met.at[t, at(c)], far.at[h, at(c)], hop2_s.at[t, c], hop2_r.at[h, c],
                      (col + blocks * (1 - t), u_in))

    def met_wait(c):
        for t in range(2):
            remote(met.at[t, at(c)], met.at[t, at(c)], hop1_s.at[t, c], hop1_r.at[t, c], inner).wait_recv()

    def far_wait(c):
        for t in range(2):
            remote(far.at[t, at(c)], far.at[t, at(c)], hop2_s.at[t, c], hop2_r.at[t, c], inner).wait_recv()

    def flatten(q, c):
        load(q, c).wait()
        wide[q] = raw[q, c].astype(F32)
        for i in range(slots):
            own[q, at(c), i * nv:(i + 1) * nv] = wide[q, pl.ds(i, size, stride=slots), :].astype(BF16)

    flatten(0, 0)
    flatten(1, 0)
    pl.semaphore_wait(barrier, 4)
    for q in range(2):
        hop1(q, 0).start()

    @pl.loop(1, AHEAD)
    def _(c):
        for q in range(2):
            flatten(q, c)
            hop1(q, c).start()

    @pl.loop(AHEAD, CHUNKS)
    def _(c):
        for q in range(2):
            flatten(q, c)

    def gram(lhs, rhs):
        return lax.dot_general(lhs, rhs, (((0,), (0,)), ((), ())), preferred_element_type=F32)

    row = lax.broadcasted_iota(jnp.int32, (size, 1), 0)

    kd[...] = jnp.zeros_like(kd)

    @pl.loop(0, CHUNKS)
    def _(c):
        kd[...] += gram(own[0, at(c)], own[0, at(c)])

    first = own[1, at(0)]
    kd[...] += gram(jnp.where(row >= over, first, jnp.zeros_like(first)), first)

    @pl.loop(1, CHUNKS)
    def _(c):
        kd[...] += gram(own[1, at(c)], own[1, at(c)])

    def half_at(w):
        return pl.ds(pl.multiple_of(w * hv, hv), hv)

    def strip_at(w):
        return pl.ds(pl.multiple_of(w * nv, nv), nv)

    kd_core = remote(kd.at[half_at(1 - s)], kd_rc, ks.at[0], kr.at[0], core)
    kd_core.start()

    vr = jnp.broadcast_to(vir[...], (nv, nv))
    vc = vr.T

    def amplitudes(m, row_occ, row_slot, col_occ, col_slot):
        energy = occ_energy[col_occ * slots + col_slot] + occ_energy[row_occ * slots + row_slot]
        live = (jnp.where(col_slot < occ_count[col_occ], 1.0, 0.0) *
                jnp.where(row_slot < occ_count[row_occ], 1.0, 0.0))
        t = m / ((energy - vr) - vc)
        return (2.0 * t - t.T) * live

    def cross(c):
        lhs, rhs = met[1, at(c)], met[0, at(c)]
        lhs = jnp.where(row + c * size >= over * h, lhs, jnp.zeros_like(lhs))
        kx[...] += gram(lhs, rhs)

    def send(item):
        @pl.when(item < CHUNKS)
        def _():
            for q in range(2):
                hop1(q, item).start()

        @pl.when(item >= CHUNKS)
        def _():
            for t in range(2):
                hop2(t, item - CHUNKS).start()

    kx[...] = jnp.zeros_like(kx)

    def met_step(c):
        met_wait(c)
        send(c + AHEAD)
        cross(c)

    met_step(0)
    kd_core.wait()
    kd_out[...] = (kd[pl.ds(pl.multiple_of(s * hv + (1 - lo) * nv, nv), nv)] + kd_rc[strip_at(1 - lo)]).astype(KSEND)
    kd_inner = remote(kd_out, kd_ri, ks.at[1], kr.at[1], inner)
    kd_inner.start()
    pl.loop(1, 4)(met_step)
    kd_inner.wait()
    mine = 2 * s + lo
    for i in range(slots):
        w = slice(i * nv, (i + 1) * nv)
        m = kd[strip_at(mine), w] + kd_rc[strip_at(lo), w] + kd_ri[:, w].astype(F32)
        td[strip_at(mine), w] = amplitudes(m, o, mine, o, i).astype(BF16)
    td_inner = remote(td.at[strip_at(mine)], td.at[strip_at(mine)], ks.at[2], kr.at[2], inner)
    td_inner.start()
    pl.loop(4, 7)(met_step)
    td_inner.wait()
    td_core = remote(td.at[half_at(s)], td.at[half_at(s)], ks.at[3], kr.at[3], core)
    td_core.start()
    pl.loop(7, CHUNKS)(met_step)

    kx_core = remote(kx.at[half_at(1 - s)], kx_rc, ks.at[4], kr.at[4], core)
    kx_core.start()
    kx_core.wait()
    for p in range(4):
        w = slice((p % 2) * hv, (p % 2 + 1) * hv)
        k = kx[pl.ds(pl.multiple_of(s * hv + (p // 2) * nv, nv), nv), w] + kx_rc[(p // 2) * nv:(p // 2 + 1) * nv, w]
        kx_out[p] = k.astype(KSEND)
        kx[pl.ds(pl.multiple_of((1 - s) * hv + (p // 2) * nv, nv), nv), w] = k
    quarters = []
    for n, (dev, p) in enumerate(((inner, 2 * h + 1 - lo), (outer, 2 * (1 - h) + 1 - lo), (diag, 2 * (1 - h) + lo))):
        quarters.append(remote(kx_out.at[p], kx_rq.at[n], ks.at[5 + n], kr.at[5 + n], dev))
        quarters[-1].start()
    far_wait(0)
    send(CHUNKS + AHEAD)
    for q in quarters:
        q.wait()
    m = kx_rq[0].astype(F32) + kx_rq[1].astype(F32) + kx_rq[2].astype(F32)
    m = m + kx[pl.ds(pl.multiple_of((1 - s) * hv + h * nv, nv), nv), pl.ds(pl.multiple_of(lo * hv, hv), hv)]
    occ_k, occ_m = col, col + blocks
    for i in range(2):
        t = amplitudes(m[:, i * nv:(i + 1) * nv], occ_m, 2 * s + h, occ_k, 2 * lo + i)
        tq[0, i] = t.astype(BF16)
        tq[1, i] = t.T.astype(BF16)
    blk[s, x] = tq[h]
    spread = []
    for n, (dev, to) in enumerate(((inner, h), (outer, 1 - h), (diag, 1 - h))):
        spread.append(remote(tq.at[to], blk.at[s, x], ks.at[8 + n], kr.at[8 + n], dev))
        spread[-1].start()
    far_wait(1)
    send(CHUNKS + AHEAD + 1)
    for q in spread:
        q.wait()
    tx_core = remote(blk.at[s], blk.at[s], ks.at[11], kr.at[11], core)
    tx_core.start()
    far_wait(2)
    send(CHUNKS + AHEAD + 2)
    tx_core.wait()
    td_core.wait()

    def tile(w):
        return slice(w * nv, (w + 1) * nv)

    @pl.when(h == 0)
    def _():
        for ss in range(2):
            for xx in range(4):
                for i in range(2):
                    tx[tile(2 * ss + xx // 2), tile(2 * (xx % 2) + i)] = blk[ss, xx, i]

    @pl.when(h == 1)
    def _():
        for ss in range(2):
            for xx in range(4):
                for i in range(2):
                    tx[tile(2 * (xx % 2) + i), tile(2 * ss + xx // 2)] = blk[ss, xx, i]

    def store(q, c, skip=0):
        at_row = slots * (q * start1 + c * size + skip)
        n = slots * (size - skip)
        return pltpu.make_async_copy(res.at[q, c, pl.ds(slots * skip, n)], out.at[pl.ds(at_row, n)], out_sem.at[q, c])

    def gamma(c, q):
        g = jnp.dot(own[q, at(c)], td[...], preferred_element_type=F32)
        g = g + jnp.dot(far[q, at(c)], tx[...], preferred_element_type=F32)
        for i in range(slots):
            wide[q, pl.ds(i, size, stride=slots), :] = g[:, i * nv:(i + 1) * nv]
        res[q, c] = wide[q].astype(BF16)

    gamma(0, 0)
    store(0, 0).start()
    gamma(0, 1)
    store(1, 0, over).start()

    @pl.loop(1, 3)
    def _(c):
        for q in range(2):
            gamma(c, q)
            store(q, c).start()

    @pl.loop(3, CHUNKS)
    def _(c):
        far_wait(c)

        @pl.when(c + AHEAD < CHUNKS)
        def _():
            for t in range(2):
                hop2(t, c + AHEAD).start()

        for q in range(2):
            gamma(c, q)
            store(q, c).start()

    @pl.loop(0, CHUNKS)
    def _(c):
        for q in range(2):
            hop1(q, c).wait_send()
            hop2(q, c).wait_send()
    store(0, 0).wait()
    store(1, 0, over).wait()

    @pl.loop(1, CHUNKS)
    def _(c):
        for q in range(2):
            store(q, c).wait()


def half_rows(rows):
    unit = 16 * CHUNKS
    return -(-(rows // 2) // unit) * unit


def on_device(b_tensor, occ_energy, vir_energy, occ_count):
    rows, slots, nv = b_tensor.shape
    flat = slots * nv
    nh = half_rows(rows)
    size = nh // CHUNKS
    dims = (lax.axis_size("occ"), rows, nv, slots)
    smem, vmem, hbm = (pl.BlockSpec(memory_space=m) for m in (pltpu.SMEM, pltpu.VMEM, pl.ANY))
    out = pl.pallas_call(
        functools.partial(kernel, dims),
        out_shape=jax.ShapeDtypeStruct((rows * slots, nv), BF16),
        in_specs=[smem, smem, vmem, hbm],
        out_specs=hbm,
        scratch_shapes=[
            pltpu.VMEM((2, CHUNKS, slots * size, nv), BF16),
            pltpu.VMEM((2, slots * size, nv), F32),
            pltpu.VMEM((2, nh, flat), BF16),
            pltpu.VMEM((2, nh, flat), BF16),
            pltpu.VMEM((2, nh, flat), BF16),
            pltpu.VMEM((2, CHUNKS, slots * size, nv), BF16),
            pltpu.VMEM((flat, flat), F32),
            pltpu.VMEM((flat, flat), F32),
            pltpu.VMEM((flat // 2, flat), F32),
            pltpu.VMEM((flat // 2, flat), F32),
            pltpu.VMEM((nv, flat), KSEND),
            pltpu.VMEM((nv, flat), KSEND),
            pltpu.VMEM((4, nv, flat // 2), KSEND),
            pltpu.VMEM((3, nv, flat // 2), KSEND),
            pltpu.VMEM((flat, flat), BF16),
            pltpu.VMEM((flat, flat), BF16),
            pltpu.VMEM((2, 2, nv, nv), BF16),
            pltpu.VMEM((2, 4, 2, nv, nv), BF16),
            pltpu.SemaphoreType.DMA((2, CHUNKS)),
            pltpu.SemaphoreType.DMA((2, CHUNKS)),
            pltpu.SemaphoreType.DMA((2, CHUNKS)),
            pltpu.SemaphoreType.DMA((2, CHUNKS)),
            pltpu.SemaphoreType.DMA((2, CHUNKS)),
            pltpu.SemaphoreType.DMA((2, CHUNKS)),
            pltpu.SemaphoreType.DMA((12,)),
            pltpu.SemaphoreType.DMA((12,)),
        ],
        compiler_params=pltpu.CompilerParams(collective_id=0, has_side_effects=True, vmem_limit_bytes=56 << 20),
    )(occ_energy, occ_count, vir_energy.reshape(1, nv), b_tensor.reshape(rows * slots, nv))
    return out.reshape(rows, slots, nv)


def solution(mesh):
    return jax.shard_map(
        on_device,
        mesh=mesh,
        in_specs=(P("aux", "occ", None), P(), P(), P()),
        out_specs=P("aux", "occ", None),
        check_vma=False,
    )
```

```python
import functools

import jax
import jax.numpy as jnp
from jax import lax
from jax.experimental import pallas as pl
from jax.experimental.pallas import tpu as pltpu
from jax.sharding import PartitionSpec as P

CHUNKS = 9
AHEAD = 2
MESH = pl.DeviceIdType.MESH
F32, BF16 = jnp.float32, jnp.bfloat16
KSEND = jnp.bfloat16


def kernel(dims, occ_energy, occ_count, vir, b, out, raw, wide, own, met, far, kd, kx, kd_rc, kx_rc,
           kd_out, kd_ri, kx_out, kx_rq, td, tx, tq, blk, load_sem, hop1_s, hop1_r, hop2_s, hop2_r,
           ks, kr):
    n_occ, rows, nv, slots = dims
    flat = slots * nv
    half = rows // 2
    size = met.shape[1] // CHUNKS
    start1 = rows - size * CHUNKS
    over = size * CHUNKS - start1
    hv = flat // 2
    o, u = lax.axis_index("occ"), lax.axis_index("aux")
    blocks = n_occ // 2
    h, col = o // blocks, o % blocks
    lo, s = u // 2, u % 2
    x = 2 * h + lo
    u_in = (u + 2) % 4
    other = (o + blocks) % n_occ
    core = (o, u + 1 - 2 * s)
    inner, outer, diag = (o, u_in), (other, u_in), (other, u)

    barrier = pltpu.get_barrier_semaphore()
    for dev in ((o, u_in), (other, u_in), (other, u), core):
        pl.semaphore_signal(barrier, inc=1, device_id=dev, device_id_type=MESH)

    def load(q, c):
        at = slots * (q * start1 + c * size)
        return pltpu.make_async_copy(b.at[pl.ds(at, slots * size)], raw.at[q, c], load_sem.at[q, c])

    for c in range(CHUNKS):
        for q in range(2):
            load(q, c).start()

    def remote(src, dst, ss, rs, dev):
        return pltpu.make_async_remote_copy(src_ref=src, dst_ref=dst, send_sem=ss, recv_sem=rs, device_id=dev,
                                            device_id_type=MESH)

    def at(c):
        return pl.ds(pl.multiple_of(c * size, 16), size)

    def hop1(q, c):
        return remote(own.at[q, at(c)], met.at[h, at(c)], hop1_s.at[q, c], hop1_r.at[h, c],
                      (col + blocks * q, u_in))

    def hop2(t, c):
        return remote(met.at[t, at(c)], far.at[h, at(c)], hop2_s.at[t, c], hop2_r.at[h, c],
                      (col + blocks * (1 - t), u_in))

    def met_wait(c):
        for t in range(2):
            remote(met.at[t, at(c)], met.at[t, at(c)], hop1_s.at[t, c], hop1_r.at[t, c], inner).wait_recv()

    def far_wait(c):
        for t in range(2):
            remote(far.at[t, at(c)], far.at[t, at(c)], hop2_s.at[t, c], hop2_r.at[t, c], inner).wait_recv()

    def flatten(q, c):
        load(q, c).wait()
        wide[q] = raw[q, c].astype(F32)
        for i in range(slots):
            own[q, at(c), i * nv:(i + 1) * nv] = wide[q, pl.ds(i, size, stride=slots), :].astype(BF16)

    flatten(0, 0)
    flatten(1, 0)
    pl.semaphore_wait(barrier, 4)
    for q in range(2):
        hop1(q, 0).start()

    @pl.loop(1, AHEAD)
    def _(c):
        for q in range(2):
            flatten(q, c)
            hop1(q, c).start()

    @pl.loop(AHEAD, CHUNKS)
    def _(c):
        for q in range(2):
            flatten(q, c)

    def gram(lhs, rhs):
        return lax.dot_general(lhs, rhs, (((0,), (0,)), ((), ())), preferred_element_type=F32)

    row = lax.broadcasted_iota(jnp.int32, (size, 1), 0)

    kd[...] = jnp.zeros_like(kd)

    @pl.loop(0, CHUNKS)
    def _(c):
        kd[...] += gram(own[0, at(c)], own[0, at(c)])

    first = own[1, at(0)]
    kd[...] += gram(jnp.where(row >= over, first, jnp.zeros_like(first)), first)

    @pl.loop(1, CHUNKS)
    def _(c):
        kd[...] += gram(own[1, at(c)], own[1, at(c)])

    def half_at(w):
        return pl.ds(pl.multiple_of(w * hv, hv), hv)

    def strip_at(w):
        return pl.ds(pl.multiple_of(w * nv, nv), nv)

    kd_core = remote(kd.at[half_at(1 - s)], kd_rc, ks.at[0], kr.at[0], core)
    kd_core.start()

    vr = jnp.broadcast_to(vir[...], (nv, nv))
    vc = vr.T

    def amplitudes(m, row_occ, row_slot, col_occ, col_slot):
        energy = occ_energy[col_occ * slots + col_slot] + occ_energy[row_occ * slots + row_slot]
        live = (jnp.where(col_slot < occ_count[col_occ], 1.0, 0.0) *
                jnp.where(row_slot < occ_count[row_occ], 1.0, 0.0))
        t = m / ((energy - vr) - vc)
        return (2.0 * t - t.T) * live

    def cross(c):
        lhs, rhs = met[1, at(c)], met[0, at(c)]
        lhs = jnp.where(row + c * size >= over * h, lhs, jnp.zeros_like(lhs))
        kx[...] += gram(lhs, rhs)

    def send(item):
        @pl.when(item < CHUNKS)
        def _():
            for q in range(2):
                hop1(q, item).start()

        @pl.when(item >= CHUNKS)
        def _():
            for t in range(2):
                hop2(t, item - CHUNKS).start()

    kx[...] = jnp.zeros_like(kx)

    def met_step(c):
        met_wait(c)
        send(c + AHEAD)
        cross(c)

    met_step(0)
    kd_core.wait()
    kd_out[...] = (kd[pl.ds(pl.multiple_of(s * hv + (1 - lo) * nv, nv), nv)] + kd_rc[strip_at(1 - lo)]).astype(KSEND)
    kd_inner = remote(kd_out, kd_ri, ks.at[1], kr.at[1], inner)
    kd_inner.start()
    pl.loop(1, 4)(met_step)
    kd_inner.wait()
    mine = 2 * s + lo
    for i in range(slots):
        w = slice(i * nv, (i + 1) * nv)
        m = kd[strip_at(mine), w] + kd_rc[strip_at(lo), w] + kd_ri[:, w].astype(F32)
        td[strip_at(mine), w] = amplitudes(m, o, mine, o, i).astype(BF16)
    td_inner = remote(td.at[strip_at(mine)], td.at[strip_at(mine)], ks.at[2], kr.at[2], inner)
    td_inner.start()
    pl.loop(4, 7)(met_step)
    td_inner.wait()
    td_core = remote(td.at[half_at(s)], td.at[half_at(s)], ks.at[3], kr.at[3], core)
    td_core.start()
    pl.loop(7, CHUNKS)(met_step)

    kx_core = remote(kx.at[half_at(1 - s)], kx_rc, ks.at[4], kr.at[4], core)
    kx_core.start()
    kx_core.wait()
    for p in range(4):
        w = slice((p % 2) * hv, (p % 2 + 1) * hv)
        k = kx[pl.ds(pl.multiple_of(s * hv + (p // 2) * nv, nv), nv), w] + kx_rc[(p // 2) * nv:(p // 2 + 1) * nv, w]
        kx_out[p] = k.astype(KSEND)
        kx[pl.ds(pl.multiple_of((1 - s) * hv + (p // 2) * nv, nv), nv), w] = k
    quarters = []
    for n, (dev, p) in enumerate(((inner, 2 * h + 1 - lo), (outer, 2 * (1 - h) + 1 - lo), (diag, 2 * (1 - h) + lo))):
        quarters.append(remote(kx_out.at[p], kx_rq.at[n], ks.at[5 + n], kr.at[5 + n], dev))
        quarters[-1].start()
    far_wait(0)
    send(CHUNKS + AHEAD)
    for q in quarters:
        q.wait()
    m = kx_rq[0].astype(F32) + kx_rq[1].astype(F32) + kx_rq[2].astype(F32)
    m = m + kx[pl.ds(pl.multiple_of((1 - s) * hv + h * nv, nv), nv), pl.ds(pl.multiple_of(lo * hv, hv), hv)]
    occ_k, occ_m = col, col + blocks
    for i in range(2):
        t = amplitudes(m[:, i * nv:(i + 1) * nv], occ_m, 2 * s + h, occ_k, 2 * lo + i)
        tq[0, i] = t.astype(BF16)
        tq[1, i] = t.T.astype(BF16)
    blk[s, x] = tq[h]
    spread = []
    for n, (dev, to) in enumerate(((inner, h), (outer, 1 - h), (diag, 1 - h))):
        spread.append(remote(tq.at[to], blk.at[s, x], ks.at[8 + n], kr.at[8 + n], dev))
        spread[-1].start()
    far_wait(1)
    send(CHUNKS + AHEAD + 1)
    for q in spread:
        q.wait()
    tx_core = remote(blk.at[s], blk.at[s], ks.at[11], kr.at[11], core)
    tx_core.start()
    far_wait(2)
    send(CHUNKS + AHEAD + 2)
    tx_core.wait()
    td_core.wait()

    def tile(w):
        return slice(w * nv, (w + 1) * nv)

    @pl.when(h == 0)
    def _():
        for ss in range(2):
            for xx in range(4):
                for i in range(2):
                    tx[tile(2 * ss + xx // 2), tile(2 * (xx % 2) + i)] = blk[ss, xx, i]

    @pl.when(h == 1)
    def _():
        for ss in range(2):
            for xx in range(4):
                for i in range(2):
                    tx[tile(2 * (xx % 2) + i), tile(2 * ss + xx // 2)] = blk[ss, xx, i]

    def gamma(c, q, skip=0):
        g = jnp.dot(own[q, at(c)], td[...], preferred_element_type=F32)
        g = g + jnp.dot(far[q, at(c)], tx[...], preferred_element_type=F32)
        for i in range(slots):
            wide[q, pl.ds(i, size, stride=slots), :] = g[:, i * nv:(i + 1) * nv]
        at_row = slots * (q * start1 + c * size + skip)
        n = slots * (size - skip)
        out[pl.ds(pl.multiple_of(at_row, 64), n)] = wide[q, slots * skip:].astype(BF16)

    gamma(0, 0)
    gamma(0, 1, over)

    @pl.loop(1, 3)
    def _(c):
        for q in range(2):
            gamma(c, q)

    @pl.loop(3, CHUNKS)
    def _(c):
        far_wait(c)

        @pl.when(c + AHEAD < CHUNKS)
        def _():
            for t in range(2):
                hop2(t, c + AHEAD).start()

        for q in range(2):
            gamma(c, q)

    @pl.loop(0, CHUNKS)
    def _(c):
        for q in range(2):
            hop1(q, c).wait_send()
            hop2(q, c).wait_send()


def half_rows(rows):
    unit = 16 * CHUNKS
    return -(-(rows // 2) // unit) * unit


def on_device(b_tensor, occ_energy, vir_energy, occ_count):
    rows, slots, nv = b_tensor.shape
    flat = slots * nv
    nh = half_rows(rows)
    size = nh // CHUNKS
    dims = (lax.axis_size("occ"), rows, nv, slots)
    smem, vmem, hbm = (pl.BlockSpec(memory_space=m) for m in (pltpu.SMEM, pltpu.VMEM, pl.ANY))
    out = pl.pallas_call(
        functools.partial(kernel, dims),
        out_shape=pltpu.VMEM((rows * slots, nv), BF16),
        in_specs=[smem, smem, vmem, hbm],
        out_specs=vmem,
        scratch_shapes=[
            pltpu.VMEM((2, CHUNKS, slots * size, nv), BF16),
            pltpu.VMEM((2, slots * size, nv), F32),
            pltpu.VMEM((2, nh, flat), BF16),
            pltpu.VMEM((2, nh, flat), BF16),
            pltpu.VMEM((2, nh, flat), BF16),
            pltpu.VMEM((flat, flat), F32),
            pltpu.VMEM((flat, flat), F32),
            pltpu.VMEM((flat // 2, flat), F32),
            pltpu.VMEM((flat // 2, flat), F32),
            pltpu.VMEM((nv, flat), KSEND),
            pltpu.VMEM((nv, flat), KSEND),
            pltpu.VMEM((4, nv, flat // 2), KSEND),
            pltpu.VMEM((3, nv, flat // 2), KSEND),
            pltpu.VMEM((flat, flat), BF16),
            pltpu.VMEM((flat, flat), BF16),
            pltpu.VMEM((2, 2, nv, nv), BF16),
            pltpu.VMEM((2, 4, 2, nv, nv), BF16),
            pltpu.SemaphoreType.DMA((2, CHUNKS)),
            pltpu.SemaphoreType.DMA((2, CHUNKS)),
            pltpu.SemaphoreType.DMA((2, CHUNKS)),
            pltpu.SemaphoreType.DMA((2, CHUNKS)),
            pltpu.SemaphoreType.DMA((2, CHUNKS)),
            pltpu.SemaphoreType.DMA((12,)),
            pltpu.SemaphoreType.DMA((12,)),
        ],
        compiler_params=pltpu.CompilerParams(collective_id=0, has_side_effects=True, vmem_limit_bytes=44 << 20),
    )(occ_energy, occ_count, vir_energy.reshape(1, nv), b_tensor.reshape(rows * slots, nv))
    return out.reshape(rows, slots, nv)


def solution(mesh):
    return jax.shard_map(
        on_device,
        mesh=mesh,
        in_specs=(P("aux", "occ", None), P(), P(), P()),
        out_specs=P("aux", "occ", None),
        check_vma=False,
    )
```

```python
import functools

import jax
import jax.numpy as jnp
from jax import lax
from jax.experimental import pallas as pl
from jax.experimental.pallas import tpu as pltpu
from jax.sharding import PartitionSpec as P

CHUNKS = 9
GROUP = 8
AHEAD = 3
MESH = pl.DeviceIdType.MESH
F32, BF16 = jnp.float32, jnp.bfloat16
CAPS = (4, 5, GROUP)
KSEND = jnp.bfloat16


def kernel(dims, cap, occ_energy, occ_count, vir, b, out, raw, wide, own, last, met, far, far_last, part, packed, crossed,
           opened, landed, kd, kx, kd_rc, kx_rc,
           kd_out, kd_ri, kx_out, kx_rq, td, tx, tq, blk, load_sem, hop1_s, hop1_r, hop2_s, hop2_r,
           ks, kr, es, er):
    n_occ, rows, nv, slots = dims
    flat = slots * nv
    most = flat - nv
    size = met.shape[1] // CHUNKS
    start1 = rows - size * CHUNKS
    over = size * CHUNKS - start1
    hv = flat // 2
    o, u = lax.axis_index("occ"), lax.axis_index("aux")
    blocks = n_occ // 2
    h, col = o // blocks, o % blocks
    lo, s = u // 2, u % 2
    x = 2 * h + lo
    u_in = (u + 2) % 4
    other = (o + blocks) % n_occ
    core = (o, u + 1 - 2 * s)
    inner, outer, diag = (o, u_in), (other, u_in), (other, u)

    barrier = pltpu.get_barrier_semaphore()
    member = col % GROUP
    base, other_base = o - member, other - member

    def mate(d):
        return (member + d) % GROUP

    for dev in (inner, outer, diag, core, *((base + mate(d), u) for d in range(1, GROUP))):
        pl.semaphore_signal(barrier, inc=1, device_id=dev, device_id_type=MESH)

    def load(q, c):
        at = slots * (q * start1 + c * size)
        return pltpu.make_async_copy(b.at[pl.ds(at, slots * size)], raw.at[q, c], load_sem.at[q, c])

    for c in range(CHUNKS):
        for q in range(2):
            load(q, c).start()

    def remote(src, dst, ss, rs, dev):
        return pltpu.make_async_remote_copy(src_ref=src, dst_ref=dst, send_sem=ss, recv_sem=rs, device_id=dev,
                                            device_id_type=MESH)

    def at(c):
        return pl.ds(pl.multiple_of(c * size, 16), size)

    def hop1(q, c):
        return remote(own.at[q, at(c)], met.at[h, at(c)], hop1_s.at[q, c], hop1_r.at[h, c],
                      (col + blocks * q, u_in))

    def hop2(t, c):
        return remote(met.at[t, at(c)], far.at[h, at(c)], hop2_s.at[t, c], hop2_r.at[h, c],
                      (col + blocks * (1 - t), u_in))

    def met_wait(c):
        for t in range(2):
            remote(met.at[t, at(c)], met.at[t, at(c)], hop1_s.at[t, c], hop1_r.at[t, c], inner).wait_recv()

    def far_wait(c):
        for t in range(2):
            remote(far.at[t, at(c)], far.at[t, at(c)], hop2_s.at[t, c], hop2_r.at[t, c], inner).wait_recv()

    def flatten(q, c):
        load(q, c).wait()
        wide[q] = raw[q, c].astype(F32)
        for i in range(slots - 1):
            own[q, at(c), i * nv:(i + 1) * nv] = wide[q, pl.ds(i, size, stride=slots), :].astype(BF16)
        last[q, at(c)] = wide[q, pl.ds(slots - 1, size, stride=slots), :].astype(BF16)

    flatten(0, 0)
    flatten(1, 0)
    pl.semaphore_wait(barrier, 4 + GROUP - 1)
    for q in range(2):
        hop1(q, 0).start()

    @pl.loop(1, AHEAD)
    def _(c):
        for q in range(2):
            flatten(q, c)
            hop1(q, c).start()

    @pl.loop(AHEAD, CHUNKS)
    def _(c):
        for q in range(2):
            flatten(q, c)

    piece = part.shape[1]
    per = GROUP // 2

    def piece_start(p):
        return (p % per) * piece - ((p % per) // (per - 1)) * (per * piece - size * CHUNKS)

    def spread(d):
        p = mate(d)
        return remote(last.at[p // per, pl.ds(pl.multiple_of(piece_start(p), 16), piece)], part.at[member],
                      es.at[0, d], er.at[0, d], (base + p, u))

    def gather(d):
        return remote(opened.at[d], landed.at[member], es.at[1, d], er.at[1, d], (base + mate(d), u))

    def place(first, j):
        n = jnp.int32(0)
        for i in range(GROUP):
            n = n + jnp.where((i < j) & (occ_count[first + i] == slots), 1, 0)
        return n

    across = remote(packed, crossed, es.at[0, 0], er.at[0, 0], diag)

    def pack():
        for d in range(1, GROUP):
            spread(d).wait()
        for p in range(cap):
            pick = jnp.int32(0)
            for j in range(GROUP):
                pick = pick + jnp.where((occ_count[base + j] == slots) & (place(base, j) == p), j, 0)
            packed[p] = part[pick]
        across.start()

    def unpack():
        across.wait()
        for d in range(GROUP):
            opened[d] = crossed[jnp.minimum(place(other_base, mate(d)), cap - 1)]
        for d in range(1, GROUP):
            gather(d).start()

    part[member] = last[member // per, pl.ds(pl.multiple_of(piece_start(member), 16), piece)]
    for d in range(1, GROUP):
        spread(d).start()

    def gram(lhs, rhs):
        return lax.dot_general(lhs, rhs, (((0,), (0,)), ((), ())), preferred_element_type=F32)

    row = lax.broadcasted_iota(jnp.int32, (size, 1), 0)

    def whole(head, tail, q, rows_at):
        return jnp.concatenate([head[q, rows_at], tail[q, rows_at]], axis=1)

    kd[...] = jnp.zeros_like(kd)

    @pl.loop(0, CHUNKS)
    def _(c):
        mine = whole(own, last, 0, at(c))
        kd[...] += gram(mine, mine)

    first = whole(own, last, 1, at(0))
    kd[...] += gram(jnp.where(row >= over, first, jnp.zeros_like(first)), first)

    @pl.loop(1, CHUNKS)
    def _(c):
        mine = whole(own, last, 1, at(c))
        kd[...] += gram(mine, mine)

    def half_at(w):
        return pl.ds(pl.multiple_of(w * hv, hv), hv)

    def strip_at(w):
        return pl.ds(pl.multiple_of(w * nv, nv), nv)

    kd_core = remote(kd.at[half_at(1 - s)], kd_rc, ks.at[0], kr.at[0], core)
    kd_core.start()

    vr = jnp.broadcast_to(vir[...], (nv, nv))
    vc = vr.T

    def amplitudes(m, row_occ, row_slot, col_occ, col_slot):
        energy = occ_energy[col_occ * slots + col_slot] + occ_energy[row_occ * slots + row_slot]
        live = (jnp.where(col_slot < occ_count[col_occ], 1.0, 0.0) *
                jnp.where(row_slot < occ_count[row_occ], 1.0, 0.0))
        t = m / ((energy - vr) - vc)
        return (2.0 * t - t.T) * live

    def cross(c):
        lhs, rhs = met[1, at(c)], met[0, at(c)]
        lhs = jnp.where(row + c * size >= over * h, lhs, jnp.zeros_like(lhs))
        kx[:most, :most] += gram(lhs, rhs)

    def send(item):
        @pl.when(item < CHUNKS)
        def _():
            for q in range(2):
                hop1(q, item).start()

        @pl.when(item >= CHUNKS)
        def _():
            for t in range(2):
                hop2(t, item - CHUNKS).start()

    kx[...] = jnp.zeros_like(kx)

    def met_step(c):
        met_wait(c)
        send(c + AHEAD)
        cross(c)

    met_step(0)
    kd_core.wait()
    kd_out[...] = (kd[pl.ds(pl.multiple_of(s * hv + (1 - lo) * nv, nv), nv)] + kd_rc[strip_at(1 - lo)]).astype(KSEND)
    kd_inner = remote(kd_out, kd_ri, ks.at[1], kr.at[1], inner)
    kd_inner.start()
    pl.loop(1, 3)(met_step)
    pack()
    met_step(3)
    kd_inner.wait()
    mine = 2 * s + lo
    for i in range(slots):
        w = slice(i * nv, (i + 1) * nv)
        m = kd[strip_at(mine), w] + kd_rc[strip_at(lo), w] + kd_ri[:, w].astype(F32)
        td[strip_at(mine), w] = amplitudes(m, o, mine, o, i).astype(BF16)
    td_inner = remote(td.at[strip_at(mine)], td.at[strip_at(mine)], ks.at[2], kr.at[2], inner)
    td_inner.start()
    pl.loop(4, 7)(met_step)
    td_inner.wait()
    td_core = remote(td.at[half_at(s)], td.at[half_at(s)], ks.at[3], kr.at[3], core)
    td_core.start()
    unpack()
    pl.loop(7, CHUNKS)(met_step)
    landed[member] = opened[0]
    for d in range(1, GROUP):
        gather(d).wait()
    for p in range(GROUP):
        far_last[p // per, pl.ds(piece_start(p), piece)] = landed[p]
    piece_row = lax.broadcasted_iota(jnp.int32, (piece, 1), 0)

    def fresh(p):
        skip = ((p % per) // (per - 1)) * (per * piece - size * CHUNKS) + (p // per) * (1 - (p % per + per - 1) // per) * over
        v = landed[p]
        return jnp.where(piece_row >= skip, v, jnp.zeros_like(v))

    @pl.when(h == 0)
    def _():
        @pl.loop(0, GROUP)
        def _(p):
            rows_at = pl.ds(pl.multiple_of(piece_start(p), 16), piece)
            kx[most:] += gram(fresh(p), whole(own, last, p // per, rows_at))

    @pl.when(h == 1)
    def _():
        @pl.loop(0, GROUP)
        def _(p):
            rows_at = pl.ds(pl.multiple_of(piece_start(p), 16), piece)
            kx[:most, most:] += gram(own[p // per, rows_at], fresh(p))


    kx_core = remote(kx.at[half_at(1 - s)], kx_rc, ks.at[4], kr.at[4], core)
    kx_core.start()
    kx_core.wait()
    for p in range(4):
        w = slice((p % 2) * hv, (p % 2 + 1) * hv)
        k = kx[pl.ds(pl.multiple_of(s * hv + (p // 2) * nv, nv), nv), w] + kx_rc[(p // 2) * nv:(p // 2 + 1) * nv, w]
        kx_out[p] = k.astype(KSEND)
        kx[pl.ds(pl.multiple_of((1 - s) * hv + (p // 2) * nv, nv), nv), w] = k
    quarters = []
    for n, (dev, p) in enumerate(((inner, 2 * h + 1 - lo), (outer, 2 * (1 - h) + 1 - lo), (diag, 2 * (1 - h) + lo))):
        quarters.append(remote(kx_out.at[p], kx_rq.at[n], ks.at[5 + n], kr.at[5 + n], dev))
        quarters[-1].start()
    far_wait(0)
    send(CHUNKS + AHEAD)
    for q in quarters:
        q.wait()
    m = kx_rq[0].astype(F32) + kx_rq[1].astype(F32) + kx_rq[2].astype(F32)
    m = m + kx[pl.ds(pl.multiple_of((1 - s) * hv + h * nv, nv), nv), pl.ds(pl.multiple_of(lo * hv, hv), hv)]
    occ_k, occ_m = col, col + blocks
    for i in range(2):
        t = amplitudes(m[:, i * nv:(i + 1) * nv], occ_m, 2 * s + h, occ_k, 2 * lo + i)
        tq[0, i] = t.astype(BF16)
        tq[1, i] = t.T.astype(BF16)
    blk[s, x] = tq[h]
    spread = []
    for n, (dev, to) in enumerate(((inner, h), (outer, 1 - h), (diag, 1 - h))):
        spread.append(remote(tq.at[to], blk.at[s, x], ks.at[8 + n], kr.at[8 + n], dev))
        spread[-1].start()
    far_wait(1)
    send(CHUNKS + AHEAD + 1)
    for q in spread:
        q.wait()
    tx_core = remote(blk.at[s], blk.at[s], ks.at[11], kr.at[11], core)
    tx_core.start()
    far_wait(2)
    send(CHUNKS + AHEAD + 2)
    tx_core.wait()
    td_core.wait()

    def tile(w):
        return slice(w * nv, (w + 1) * nv)

    @pl.when(h == 0)
    def _():
        for ss in range(2):
            for xx in range(4):
                for i in range(2):
                    tx[tile(2 * ss + xx // 2), tile(2 * (xx % 2) + i)] = blk[ss, xx, i]

    @pl.when(h == 1)
    def _():
        for ss in range(2):
            for xx in range(4):
                for i in range(2):
                    tx[tile(2 * (xx % 2) + i), tile(2 * ss + xx // 2)] = blk[ss, xx, i]

    def gamma(c, q, skip=0):
        g = jnp.dot(whole(own, last, q, at(c)), td[...], preferred_element_type=F32)
        g = g + jnp.dot(whole(far, far_last, q, at(c)), tx[...], preferred_element_type=F32)
        for i in range(slots):
            wide[q, pl.ds(i, size, stride=slots), :] = g[:, i * nv:(i + 1) * nv]
        at_row = slots * (q * start1 + c * size + skip)
        n = slots * (size - skip)
        out[pl.ds(pl.multiple_of(at_row, 64), n)] = wide[q, slots * skip:].astype(BF16)

    gamma(0, 0)
    gamma(0, 1, over)

    @pl.loop(1, 3)
    def _(c):
        for q in range(2):
            gamma(c, q)

    @pl.loop(3, CHUNKS)
    def _(c):
        far_wait(c)

        @pl.when(c + AHEAD < CHUNKS)
        def _():
            for t in range(2):
                hop2(t, c + AHEAD).start()

        for q in range(2):
            gamma(c, q)

    @pl.loop(0, CHUNKS)
    def _(c):
        for q in range(2):
            hop1(q, c).wait_send()
            hop2(q, c).wait_send()


def half_rows(rows):
    unit = 16 * CHUNKS
    return -(-(rows // 2) // unit) * unit


def on_device(b_tensor, occ_energy, vir_energy, occ_count):
    rows, slots, nv = b_tensor.shape
    flat = slots * nv
    nh = half_rows(rows)
    size = nh // CHUNKS
    dims = (lax.axis_size("occ"), rows, nv, slots)
    smem, vmem, hbm = (pl.BlockSpec(memory_space=m) for m in (pltpu.SMEM, pltpu.VMEM, pl.ANY))
    piece = -(-nh // (GROUP // 2) // 16) * 16

    def run(number, cap):
        return pl.pallas_call(
            functools.partial(kernel, dims, cap),
            out_shape=pltpu.VMEM((rows * slots, nv), BF16),
            in_specs=[smem, smem, vmem, hbm],
            out_specs=vmem,
            scratch_shapes=[
                pltpu.VMEM((2, CHUNKS, slots * size, nv), BF16),
                pltpu.VMEM((2, slots * size, nv), F32),
                pltpu.VMEM((2, nh, flat - nv), BF16),
                pltpu.VMEM((2, nh, nv), BF16),
                pltpu.VMEM((2, nh, flat - nv), BF16),
                pltpu.VMEM((2, nh, flat - nv), BF16),
                pltpu.VMEM((2, nh, nv), BF16),
                pltpu.VMEM((GROUP, piece, nv), BF16),
                pltpu.VMEM((cap, piece, nv), BF16),
                pltpu.VMEM((cap, piece, nv), BF16),
                pltpu.VMEM((GROUP, piece, nv), BF16),
                pltpu.VMEM((GROUP, piece, nv), BF16),
                pltpu.VMEM((flat, flat), F32),
                pltpu.VMEM((flat, flat), F32),
                pltpu.VMEM((flat // 2, flat), F32),
                pltpu.VMEM((flat // 2, flat), F32),
                pltpu.VMEM((nv, flat), KSEND),
                pltpu.VMEM((nv, flat), KSEND),
                pltpu.VMEM((4, nv, flat // 2), KSEND),
                pltpu.VMEM((3, nv, flat // 2), KSEND),
                pltpu.VMEM((flat, flat), BF16),
                pltpu.VMEM((flat, flat), BF16),
                pltpu.VMEM((2, 2, nv, nv), BF16),
                pltpu.VMEM((2, 4, 2, nv, nv), BF16),
                pltpu.SemaphoreType.DMA((2, CHUNKS)),
                pltpu.SemaphoreType.DMA((2, CHUNKS)),
                pltpu.SemaphoreType.DMA((2, CHUNKS)),
                pltpu.SemaphoreType.DMA((2, CHUNKS)),
                pltpu.SemaphoreType.DMA((2, CHUNKS)),
                pltpu.SemaphoreType.DMA((12,)),
                pltpu.SemaphoreType.DMA((12,)),
                pltpu.SemaphoreType.DMA((2, GROUP)),
                pltpu.SemaphoreType.DMA((2, GROUP)),
            ],
            compiler_params=pltpu.CompilerParams(collective_id=number, has_side_effects=True,
                                                 vmem_limit_bytes=46 << 20),
        )(occ_energy, occ_count, vir_energy.reshape(1, nv), b_tensor.reshape(rows * slots, nv))

    full = (occ_count == slots).astype(jnp.int32).reshape(-1, GROUP).sum(axis=1).max()
    which = sum((full > cap).astype(jnp.int32) for cap in CAPS[:-1])
    out = lax.switch(which, [functools.partial(run, n, cap) for n, cap in enumerate(CAPS)])
    return out.reshape(rows, slots, nv)


def solution(mesh):
    return jax.shard_map(
        on_device,
        mesh=mesh,
        in_specs=(P("aux", "occ", None), P(), P(), P()),
        out_specs=P("aux", "occ", None),
        check_vma=False,
    )
```

```python
import functools

import jax
import jax.numpy as jnp
from jax import lax
from jax.experimental import pallas as pl
from jax.experimental.pallas import tpu as pltpu
from jax.sharding import PartitionSpec as P

CHUNKS = 9
GROUP = 8
AHEAD = 3
MESH = pl.DeviceIdType.MESH
F32, BF16 = jnp.float32, jnp.bfloat16
CAPS = (3, 4, 5, GROUP)
STEPS = (0, 5, 2, 6, 8, 7, 8, 9, 10, 11)
KSEND = jnp.bfloat16


def kernel(dims, cap, occ_energy, occ_count, vir, b, out, raw, wide, own, last, met, far, far_last, part, packed, crossed,
           opened, landed, kd, kx, kd_rc, kx_rc,
           kd_out, kd_ri, kx_out, kx_rq, td, tx, tq, blk, kd_up, td_up, load_sem, hop1_s, hop1_r, hop2_s, hop2_r,
           ks, kr, es, er):
    n_occ, rows, nv, slots = dims
    flat = slots * nv
    most = flat - nv
    size = met.shape[1] // CHUNKS
    start1 = rows - size * CHUNKS
    over = size * CHUNKS - start1
    hv = flat // 2
    o, u = lax.axis_index("occ"), lax.axis_index("aux")
    blocks = n_occ // 2
    h, col = o // blocks, o % blocks
    lo, s = u // 2, u % 2
    x = 2 * h + lo
    u_in = (u + 2) % 4
    other = (o + blocks) % n_occ
    core = (o, u + 1 - 2 * s)
    inner, outer, diag = (o, u_in), (other, u_in), (other, u)

    barrier = pltpu.get_barrier_semaphore()
    member = col % GROUP
    base, other_base = o - member, other - member

    def mate(d):
        return (member + d) % GROUP

    for dev in (inner, outer, diag, core, *((base + mate(d), u) for d in range(1, GROUP))):
        pl.semaphore_signal(barrier, inc=1, device_id=dev, device_id_type=MESH)

    def load(q, c):
        at = slots * (q * start1 + c * size)
        return pltpu.make_async_copy(b.at[pl.ds(at, slots * size)], raw.at[q, c], load_sem.at[q, c])

    for q in range(2):
        load(q, 0).start()

    def remote(src, dst, ss, rs, dev):
        return pltpu.make_async_remote_copy(src_ref=src, dst_ref=dst, send_sem=ss, recv_sem=rs, device_id=dev,
                                            device_id_type=MESH)

    def at(c):
        return pl.ds(pl.multiple_of(c * size, 16), size)

    def hop1(q, c):
        return remote(own.at[q, at(c)], met.at[h, at(c)], hop1_s.at[q, c], hop1_r.at[h, c],
                      (col + blocks * q, u_in))

    def hop2(t, c):
        return remote(met.at[t, at(c)], far.at[h, at(c)], hop2_s.at[t, c], hop2_r.at[h, c],
                      (col + blocks * (1 - t), u_in))

    def met_wait(c):
        for t in range(2):
            remote(met.at[t, at(c)], met.at[t, at(c)], hop1_s.at[t, c], hop1_r.at[t, c], inner).wait_recv()

    def far_wait(c):
        for t in range(2):
            remote(far.at[t, at(c)], far.at[t, at(c)], hop2_s.at[t, c], hop2_r.at[t, c], inner).wait_recv()

    def flatten(q, c):
        load(q, c).wait()
        wide[q] = raw[q, c].astype(F32)
        for i in range(slots - 1):
            own[q, at(c), i * nv:(i + 1) * nv] = wide[q, pl.ds(i, size, stride=slots), :].astype(BF16)
        last[q, at(c)] = wide[q, pl.ds(slots - 1, size, stride=slots), :].astype(BF16)

    flatten(0, 0)
    flatten(1, 0)
    pl.semaphore_wait(barrier, 4 + GROUP - 1)
    for q in range(2):
        hop1(q, 0).start()
    for c in range(1, CHUNKS):
        for q in range(2):
            load(q, c).start()

    @pl.loop(1, AHEAD)
    def _(c):
        for q in range(2):
            flatten(q, c)
            hop1(q, c).start()

    @pl.loop(AHEAD, CHUNKS)
    def _(c):
        for q in range(2):
            flatten(q, c)

    piece = part.shape[1]
    per = GROUP // 2

    def piece_start(p):
        return (p % per) * piece - ((p % per) // (per - 1)) * (per * piece - size * CHUNKS)

    def spread(d):
        p = mate(d)
        return remote(last.at[p // per, pl.ds(pl.multiple_of(piece_start(p), 16), piece)], part.at[member],
                      es.at[0, d], er.at[0, d], (base + p, u))

    def gather(d):
        return remote(opened.at[mate(d)], landed.at[member], es.at[1, d], er.at[1, d], (base + mate(d), u))

    def places(first):
        n, found = jnp.int32(0), []
        for j in range(GROUP):
            one = jnp.where(occ_count[first + j] == slots, 1, 0)
            found.append((one, n))
            n = n + one
        return found

    across = remote(packed, crossed, es.at[0, 0], er.at[0, 0], diag)

    def pack():
        @pl.loop(1, GROUP)
        def _(d):
            spread(d).wait()

        found = places(base)
        for p in range(cap):
            pick = jnp.int32(0)
            for j, (one, n) in enumerate(found):
                pick = pick + jnp.where(n == p, one * j, 0)
            packed[p] = part[pick]
        across.start()

    def unpack():
        across.wait()
        for j, (_, n) in enumerate(places(other_base)):
            opened[j] = crossed[jnp.minimum(n, cap - 1)]

        @pl.loop(1, GROUP)
        def _(d):
            gather(d).start()

    part[member] = last[member // per, pl.ds(pl.multiple_of(piece_start(member), 16), piece)]

    @pl.loop(1, GROUP)
    def _(d):
        spread(d).start()

    def gram(lhs, rhs):
        return lax.dot_general(lhs, rhs, (((0,), (0,)), ((), ())), preferred_element_type=F32)

    row = lax.broadcasted_iota(jnp.int32, (size, 1), 0)

    def whole(head, tail, q, rows_at):
        return jnp.concatenate([head[q, rows_at], tail[q, rows_at]], axis=1)

    kd[...] = jnp.zeros_like(kd)

    @pl.loop(0, CHUNKS)
    def _(c):
        mine = whole(own, last, 0, at(c))
        kd[...] += gram(mine, mine)

    first = whole(own, last, 1, at(0))
    kd[...] += gram(jnp.where(row >= over, first, jnp.zeros_like(first)), first)

    @pl.loop(1, CHUNKS)
    def _(c):
        mine = whole(own, last, 1, at(c))
        kd[...] += gram(mine, mine)

    def tile(w):
        return slice(w * nv, (w + 1) * nv)

    upper = [(j, i) for j in range(slots) for i in range(j, slots)]
    split = len(upper) // 2
    for n, (j, i) in enumerate(upper):
        kd_up[n // split, n % split] = kd[tile(j), tile(i)]

    def half_at(w):
        return pl.ds(pl.multiple_of(w * hv, hv), hv)

    kd_core = remote(kd_up.at[1 - s], kd_rc, ks.at[0], kr.at[0], core)
    kd_core.start()

    vr = jnp.broadcast_to(vir[...], (nv, nv))
    vc = vr.T

    def amplitudes(m, row_occ, row_slot, col_occ, col_slot):
        energy = occ_energy[col_occ * slots + col_slot] + occ_energy[row_occ * slots + row_slot]
        live = (jnp.where(col_slot < occ_count[col_occ], 1.0, 0.0) *
                jnp.where(row_slot < occ_count[row_occ], 1.0, 0.0))
        t = m / ((energy - vr) - vc)
        return (2.0 * t - t.T) * live

    def cross(c):
        lhs, rhs = met[1, at(c)], met[0, at(c)]
        lhs = jnp.where(row + c * size >= over * h, lhs, jnp.zeros_like(lhs))
        kx[:most, :most] += gram(lhs, rhs)

    def send(item):
        @pl.when(item < CHUNKS)
        def _():
            for q in range(2):
                hop1(q, item).start()

        @pl.when(item >= CHUNKS)
        def _():
            for t in range(2):
                hop2(t, item - CHUNKS).start()

    kx[...] = jnp.zeros_like(kx)

    def met_step(c):
        met_wait(c)
        send(c + AHEAD)
        cross(c)

    kd_inner = remote(kd_out, kd_ri, ks.at[1], kr.at[1], inner)
    td_core = remote(td_up.at[s], td_up.at[s], ks.at[3], kr.at[3], core)

    def diag_send():
        kd_core.wait()
        kd_out[...] = (kd_up[s] + kd_rc[...]).astype(KSEND)
        kd_inner.start()

    def diag_tiles():
        kd_inner.wait()
        for n in range(split):
            (j, i), (jj, ii) = upper[n], upper[n + split]
            m = kd_up[s, n] + kd_rc[n] + kd_ri[n].astype(F32)
            td_up[s, n] = amplitudes(m, o, j + s * (jj - j), o, i + s * (ii - i)).astype(BF16)
        td_core.start()

    def diag_place():
        td_core.wait()
        for n, (j, i) in enumerate(upper):
            t = td_up[n // split, n % split]
            td[tile(j), tile(i)] = t
            if j != i:
                td[tile(i), tile(j)] = t.astype(F32).T.astype(BF16)

    def land():
        landed[member] = opened[member]

        @pl.loop(1, GROUP)
        def _(d):
            gather(d).wait()

        @pl.loop(0, GROUP)
        def _(p):
            far_last[p // per, pl.ds(pl.multiple_of(piece_start(p), 16), piece)] = landed[p]

        big = 3 * size
        big_row = lax.broadcasted_iota(jnp.int32, (big, 1), 0)

        def fresh(c):
            v = far_last[c // (CHUNKS // 3), big_at(c)]
            return jnp.where((big_row >= over) | (c != CHUNKS // 3), v, jnp.zeros_like(v))

        def big_at(c):
            return pl.ds(pl.multiple_of((c % (CHUNKS // 3)) * big, 16), big)

        @pl.when(h == 0)
        def _():
            @pl.loop(0, 2 * CHUNKS // 3)
            def _(c):
                kx[most:] += gram(fresh(c), whole(own, last, c // (CHUNKS // 3), big_at(c)))

        @pl.when(h == 1)
        def _():
            @pl.loop(0, 2 * CHUNKS // 3)
            def _(c):
                kx[:most, most:] += gram(own[c // (CHUNKS // 3), big_at(c)], fresh(c))

    kx_core = remote(kx.at[half_at(1 - s)], kx_rc, ks.at[4], kr.at[4], core)
    quarters = [remote(kx_out.at[p], kx_rq.at[n], ks.at[5 + n], kr.at[5 + n], dev) for n, (dev, p) in enumerate(
        ((inner, 2 * h + 1 - lo), (outer, 2 * (1 - h) + 1 - lo), (diag, 2 * (1 - h) + lo)))]
    shares = [remote(tq.at[to], blk.at[s, x], ks.at[8 + n], kr.at[8 + n], dev) for n, (dev, to) in enumerate(
        ((inner, h), (outer, 1 - h), (diag, 1 - h)))]
    tx_core = remote(blk.at[s], blk.at[s], ks.at[11], kr.at[11], core)

    def cross_send():
        kx_core.start()
        kx_core.wait()
        for p in range(4):
            w = slice((p % 2) * hv, (p % 2 + 1) * hv)
            k = kx[pl.ds(pl.multiple_of(s * hv + (p // 2) * nv, nv), nv), w] + kx_rc[tile(p // 2), w]
            kx_out[p] = k.astype(KSEND)
            kx[pl.ds(pl.multiple_of((1 - s) * hv + (p // 2) * nv, nv), nv), w] = k
        for q in quarters:
            q.start()

    def cross_tiles():
        for q in quarters:
            q.wait()
        m = kx_rq[0].astype(F32) + kx_rq[1].astype(F32) + kx_rq[2].astype(F32)
        m = m + kx[pl.ds(pl.multiple_of((1 - s) * hv + h * nv, nv), nv), pl.ds(pl.multiple_of(lo * hv, hv), hv)]
        occ_k, occ_m = col, col + blocks
        for i in range(2):
            t = amplitudes(m[:, i * nv:(i + 1) * nv], occ_m, 2 * s + h, occ_k, 2 * lo + i)
            tq[0, i] = t.astype(BF16)
            tq[1, i] = t.T.astype(BF16)
        blk[s, x] = tq[h]
        for q in shares:
            q.start()

    def cross_swap():
        for q in shares:
            q.wait()
        tx_core.start()

    def cross_place():
        tx_core.wait()

        @pl.when(h == 0)
        def _():
            for ss in range(2):
                for xx in range(4):
                    for i in range(2):
                        tx[tile(2 * ss + xx // 2), tile(2 * (xx % 2) + i)] = blk[ss, xx, i]

        @pl.when(h == 1)
        def _():
            for ss in range(2):
                for xx in range(4):
                    for i in range(2):
                        tx[tile(2 * (xx % 2) + i), tile(2 * ss + xx // 2)] = blk[ss, xx, i]

    after = {}
    for step, todo in zip(STEPS, (diag_send, diag_tiles, pack, unpack, land, diag_place, cross_send, cross_tiles,
                                  cross_swap, cross_place), strict=True):
        after.setdefault(step, []).append(todo)
    begin = 0
    for step in sorted(after):
        if step < CHUNKS:
            pl.loop(begin, step + 1)(met_step)
        else:
            if begin < CHUNKS:
                pl.loop(begin, CHUNKS)(met_step)
            for c in range(max(begin, CHUNKS), step + 1):
                far_wait(c - CHUNKS)
                if c + AHEAD < 2 * CHUNKS:
                    send(c + AHEAD)
        begin = step + 1
        for todo in after[step]:
            todo()
    ready = begin - CHUNKS

    def gamma(c, q, skip=0):
        g = jnp.dot(whole(own, last, q, at(c)), td[...], preferred_element_type=F32)
        g = g + jnp.dot(whole(far, far_last, q, at(c)), tx[...], preferred_element_type=F32)
        for i in range(slots):
            wide[q, pl.ds(i, size, stride=slots), :] = g[:, i * nv:(i + 1) * nv]
        at_row = slots * (q * start1 + c * size + skip)
        n = slots * (size - skip)
        out[pl.ds(pl.multiple_of(at_row, 64), n)] = wide[q, slots * skip:].astype(BF16)

    gamma(0, 0)
    gamma(0, 1, over)

    @pl.loop(1, ready)
    def _(c):
        for q in range(2):
            gamma(c, q)

    @pl.loop(ready, CHUNKS)
    def _(c):
        far_wait(c)

        @pl.when(c + AHEAD < CHUNKS)
        def _():
            for t in range(2):
                hop2(t, c + AHEAD).start()

        for q in range(2):
            gamma(c, q)

    @pl.loop(0, CHUNKS)
    def _(c):
        for q in range(2):
            hop1(q, c).wait_send()
            hop2(q, c).wait_send()


def half_rows(rows):
    unit = 16 * CHUNKS
    return -(-(rows // 2) // unit) * unit


def on_device(b_tensor, occ_energy, vir_energy, occ_count):
    rows, slots, nv = b_tensor.shape
    flat = slots * nv
    nh = half_rows(rows)
    size = nh // CHUNKS
    dims = (lax.axis_size("occ"), rows, nv, slots)
    smem, vmem, hbm = (pl.BlockSpec(memory_space=m) for m in (pltpu.SMEM, pltpu.VMEM, pl.ANY))
    half_up = slots * (slots + 1) // 4
    piece = -(-nh // (GROUP // 2) // 16) * 16

    def run(number, cap):
        return pl.pallas_call(
            functools.partial(kernel, dims, cap),
            out_shape=pltpu.VMEM((rows * slots, nv), BF16),
            in_specs=[smem, smem, vmem, hbm],
            out_specs=vmem,
            scratch_shapes=[
                pltpu.VMEM((2, CHUNKS, slots * size, nv), BF16),
                pltpu.VMEM((2, slots * size, nv), F32),
                pltpu.VMEM((2, nh, flat - nv), BF16),
                pltpu.VMEM((2, nh, nv), BF16),
                pltpu.VMEM((2, nh, flat - nv), BF16),
                pltpu.VMEM((2, nh, flat - nv), BF16),
                pltpu.VMEM((2, nh, nv), BF16),
                pltpu.VMEM((GROUP, piece, nv), BF16),
                pltpu.VMEM((cap, piece, nv), BF16),
                pltpu.VMEM((cap, piece, nv), BF16),
                pltpu.VMEM((GROUP, piece, nv), BF16),
                pltpu.VMEM((GROUP, piece, nv), BF16),
                pltpu.VMEM((flat, flat), F32),
                pltpu.VMEM((flat, flat), F32),
                pltpu.VMEM((half_up, nv, nv), F32),
                pltpu.VMEM((flat // 2, flat), F32),
                pltpu.VMEM((half_up, nv, nv), KSEND),
                pltpu.VMEM((half_up, nv, nv), KSEND),
                pltpu.VMEM((4, nv, flat // 2), KSEND),
                pltpu.VMEM((3, nv, flat // 2), KSEND),
                pltpu.VMEM((flat, flat), BF16),
                pltpu.VMEM((flat, flat), BF16),
                pltpu.VMEM((2, 2, nv, nv), BF16),
                pltpu.VMEM((2, 4, 2, nv, nv), BF16),
                pltpu.VMEM((2, half_up, nv, nv), F32),
                pltpu.VMEM((2, half_up, nv, nv), BF16),
                pltpu.SemaphoreType.DMA((2, CHUNKS)),
                pltpu.SemaphoreType.DMA((2, CHUNKS)),
                pltpu.SemaphoreType.DMA((2, CHUNKS)),
                pltpu.SemaphoreType.DMA((2, CHUNKS)),
                pltpu.SemaphoreType.DMA((2, CHUNKS)),
                pltpu.SemaphoreType.DMA((12,)),
                pltpu.SemaphoreType.DMA((12,)),
                pltpu.SemaphoreType.DMA((2, GROUP)),
                pltpu.SemaphoreType.DMA((2, GROUP)),
            ],
            compiler_params=pltpu.CompilerParams(collective_id=number, has_side_effects=True,
                                                 vmem_limit_bytes=46 << 20),
        )(occ_energy, occ_count, vir_energy.reshape(1, nv), b_tensor.reshape(rows * slots, nv))

    full = (occ_count == slots).astype(jnp.int32).reshape(-1, GROUP).sum(axis=1)
    which = sum((full > cap).astype(jnp.int32) for cap in CAPS[:-1]).max()
    out = lax.switch(which, [functools.partial(run, n, cap) for n, cap in enumerate(CAPS)])
    return out.reshape(rows, slots, nv)


def solution(mesh):
    return jax.shard_map(
        on_device,
        mesh=mesh,
        in_specs=(P("aux", "occ", None), P(), P(), P()),
        out_specs=P("aux", "occ", None),
        check_vma=False,
    )
```

```python
import functools

import jax
import jax.numpy as jnp
from jax import lax
from jax.experimental import pallas as pl
from jax.experimental.pallas import tpu as pltpu
from jax.sharding import PartitionSpec as P

CHUNKS = 9
GROUP = 8
AHEAD = 4
MESH = pl.DeviceIdType.MESH
F32, BF16 = jnp.float32, jnp.bfloat16
CAPS = (3, 4, 5, GROUP)
STEPS = (0, 5, 2, 6, 8, 7, 8, 9, 10, 11, 12, 13)
KSEND = jnp.bfloat16


def kernel(dims, cap, occ_energy, occ_count, vir, b, out, raw, wide, own, last, met, far, far_last, part, packed, crossed,
           opened, landed, kd, kx, kd_rc, kx_rc,
           kd_out, kd_ri, kx_out, kx_ro, kx_half, kx_ri, td, tx, tq, turned, blk, kd_up, td_up, load_sem, hop1_s, hop1_r, hop2_s, hop2_r,
           ks, kr, es, er):
    n_occ, rows, nv, slots = dims
    flat = slots * nv
    most = flat - nv
    size = met.shape[1] // CHUNKS
    start1 = rows - size * CHUNKS
    over = size * CHUNKS - start1
    hv = flat // 2
    o, u = lax.axis_index("occ"), lax.axis_index("aux")
    blocks = n_occ // 2
    h, col = o // blocks, o % blocks
    lo, s = u // 2, u % 2
    x = 2 * h + lo
    u_in = (u + 2) % 4
    other = (o + blocks) % n_occ
    core = (o, u + 1 - 2 * s)
    inner, outer, diag = (o, u_in), (other, u_in), (other, u)

    barrier = pltpu.get_barrier_semaphore()
    member = col % GROUP
    base, other_base = o - member, other - member

    def mate(d):
        return (member + d) % GROUP

    for dev in (inner, outer, diag, core, *((base + mate(d), u) for d in range(1, GROUP))):
        pl.semaphore_signal(barrier, inc=1, device_id=dev, device_id_type=MESH)

    def load(q, c):
        at = slots * (q * start1 + c * size)
        return pltpu.make_async_copy(b.at[pl.ds(at, slots * size)], raw.at[q, c], load_sem.at[q, c])

    for q in range(2):
        load(q, 0).start()

    def remote(src, dst, ss, rs, dev):
        return pltpu.make_async_remote_copy(src_ref=src, dst_ref=dst, send_sem=ss, recv_sem=rs, device_id=dev,
                                            device_id_type=MESH)

    def at(c):
        return pl.ds(pl.multiple_of(c * size, 16), size)

    def hop1(q, c):
        return remote(own.at[q, at(c)], met.at[h, at(c)], hop1_s.at[q, c], hop1_r.at[h, c],
                      (col + blocks * q, u_in))

    def hop2(t, c):
        return remote(met.at[t, at(c)], far.at[h, at(c)], hop2_s.at[t, c], hop2_r.at[h, c],
                      (col + blocks * (1 - t), u_in))

    def met_wait(c):
        for t in range(2):
            remote(met.at[t, at(c)], met.at[t, at(c)], hop1_s.at[t, c], hop1_r.at[t, c], inner).wait_recv()

    def far_wait(c):
        for t in range(2):
            remote(far.at[t, at(c)], far.at[t, at(c)], hop2_s.at[t, c], hop2_r.at[t, c], inner).wait_recv()

    def flatten(q, c):
        load(q, c).wait()
        wide[q] = raw[q, c].astype(F32)
        for i in range(slots - 1):
            own[q, at(c), i * nv:(i + 1) * nv] = wide[q, pl.ds(i, size, stride=slots), :].astype(BF16)
        last[q, at(c)] = wide[q, pl.ds(slots - 1, size, stride=slots), :].astype(BF16)

    flatten(0, 0)
    flatten(1, 0)
    pl.semaphore_wait(barrier, 4 + GROUP - 1)
    for q in range(2):
        hop1(q, 0).start()
    for c in range(1, CHUNKS):
        for q in range(2):
            load(q, c).start()

    @pl.loop(1, AHEAD)
    def _(c):
        for q in range(2):
            flatten(q, c)
            hop1(q, c).start()

    @pl.loop(AHEAD, CHUNKS)
    def _(c):
        for q in range(2):
            flatten(q, c)

    piece = part.shape[1]
    per = GROUP // 2

    def piece_start(p):
        return (p % per) * piece - ((p % per) // (per - 1)) * (per * piece - size * CHUNKS)

    def spread(d):
        p = mate(d)
        return remote(last.at[p // per, pl.ds(pl.multiple_of(piece_start(p), 16), piece)], part.at[member],
                      es.at[0, d], er.at[0, d], (base + p, u))

    def gather(d):
        return remote(opened.at[mate(d)], landed.at[member], es.at[1, d], er.at[1, d], (base + mate(d), u))

    def places(first):
        n, found = jnp.int32(0), []
        for j in range(GROUP):
            one = jnp.where(occ_count[first + j] == slots, 1, 0)
            found.append((one, n))
            n = n + one
        return found

    across = remote(packed, crossed, es.at[0, 0], er.at[0, 0], diag)

    def pack():
        @pl.loop(1, GROUP)
        def _(d):
            spread(d).wait()

        found = places(base)
        for p in range(cap):
            pick = jnp.int32(0)
            for j, (one, n) in enumerate(found):
                pick = pick + jnp.where(n == p, one * j, 0)
            packed[p] = part[pick]
        across.start()

    def unpack():
        across.wait()
        for j, (_, n) in enumerate(places(other_base)):
            opened[j] = crossed[jnp.minimum(n, cap - 1)]

        @pl.loop(1, GROUP)
        def _(d):
            gather(d).start()

    part[member] = last[member // per, pl.ds(pl.multiple_of(piece_start(member), 16), piece)]

    @pl.loop(1, GROUP)
    def _(d):
        spread(d).start()

    def gram(lhs, rhs):
        return lax.dot_general(lhs, rhs, (((0,), (0,)), ((), ())), preferred_element_type=F32)

    row = lax.broadcasted_iota(jnp.int32, (size, 1), 0)

    def whole(head, tail, q, rows_at):
        return jnp.concatenate([head[q, rows_at], tail[q, rows_at]], axis=1)

    kd[...] = jnp.zeros_like(kd)

    @pl.loop(0, CHUNKS)
    def _(c):
        mine = whole(own, last, 0, at(c))
        kd[...] += gram(mine, mine)

    first = whole(own, last, 1, at(0))
    kd[...] += gram(jnp.where(row >= over, first, jnp.zeros_like(first)), first)

    @pl.loop(1, CHUNKS)
    def _(c):
        mine = whole(own, last, 1, at(c))
        kd[...] += gram(mine, mine)

    def tile(w):
        return slice(w * nv, (w + 1) * nv)

    upper = [(j, i) for j in range(slots) for i in range(j, slots)]
    split = len(upper) // 2
    for n, (j, i) in enumerate(upper):
        kd_up[n // split, n % split] = kd[tile(j), tile(i)]

    def half_at(w):
        return pl.ds(pl.multiple_of(w * hv, hv), hv)

    kd_core = remote(kd_up.at[1 - s], kd_rc, ks.at[0], kr.at[0], core)
    kd_core.start()

    vr = jnp.broadcast_to(vir[...], (nv, nv))
    vc = vr.T

    def amplitudes(m, row_occ, row_slot, col_occ, col_slot):
        energy = occ_energy[col_occ * slots + col_slot] + occ_energy[row_occ * slots + row_slot]
        live = (jnp.where(col_slot < occ_count[col_occ], 1.0, 0.0) *
                jnp.where(row_slot < occ_count[row_occ], 1.0, 0.0))
        t = m / ((energy - vr) - vc)
        return (2.0 * t - t.T) * live

    def cross(c):
        lhs, rhs = met[1, at(c)], met[0, at(c)]
        lhs = jnp.where(row + c * size >= over * h, lhs, jnp.zeros_like(lhs))
        kx[:most, :most] += gram(lhs, rhs)

    def send(item):
        @pl.when(item < CHUNKS)
        def _():
            for q in range(2):
                hop1(q, item).start()

        @pl.when(item >= CHUNKS)
        def _():
            for t in range(2):
                hop2(t, item - CHUNKS).start()

    kx[...] = jnp.zeros_like(kx)

    def met_step(c):
        met_wait(c)
        send(c + AHEAD)
        cross(c)

    kd_inner = remote(kd_out, kd_ri, ks.at[1], kr.at[1], inner)
    td_core = remote(td_up.at[s], td_up.at[s], ks.at[3], kr.at[3], core)

    def diag_send():
        kd_core.wait()
        kd_out[...] = (kd_up[s] + kd_rc[...]).astype(KSEND)
        kd_inner.start()

    def diag_tiles():
        kd_inner.wait()
        for n in range(split):
            (j, i), (jj, ii) = upper[n], upper[n + split]
            m = kd_up[s, n] + kd_rc[n] + kd_ri[n].astype(F32)
            td_up[s, n] = amplitudes(m, o, j + s * (jj - j), o, i + s * (ii - i)).astype(BF16)
        td_core.start()

    def diag_place():
        td_core.wait()
        for n, (j, i) in enumerate(upper):
            t = td_up[n // split, n % split]
            td[tile(j), tile(i)] = t
            if j != i:
                td[tile(i), tile(j)] = t.astype(F32).T.astype(BF16)

    def land():
        landed[member] = opened[member]

        @pl.loop(1, GROUP)
        def _(d):
            gather(d).wait()

        @pl.loop(0, GROUP)
        def _(p):
            far_last[p // per, pl.ds(pl.multiple_of(piece_start(p), 16), piece)] = landed[p]

        big = 3 * size
        big_row = lax.broadcasted_iota(jnp.int32, (big, 1), 0)

        def fresh(c):
            v = far_last[c // (CHUNKS // 3), big_at(c)]
            return jnp.where((big_row >= over) | (c != CHUNKS // 3), v, jnp.zeros_like(v))

        def big_at(c):
            return pl.ds(pl.multiple_of((c % (CHUNKS // 3)) * big, 16), big)

        @pl.when(h == 0)
        def _():
            @pl.loop(0, 2 * CHUNKS // 3)
            def _(c):
                kx[most:] += gram(fresh(c), whole(own, last, c // (CHUNKS // 3), big_at(c)))

        @pl.when(h == 1)
        def _():
            @pl.loop(0, 2 * CHUNKS // 3)
            def _(c):
                kx[:most, most:] += gram(own[c // (CHUNKS // 3), big_at(c)], fresh(c))

    kx_core = remote(kx.at[half_at(1 - s)], kx_rc, ks.at[4], kr.at[4], core)
    kx_outer = remote(kx_out.at[pl.ds(2 * (1 - h), 2)], kx_ro, ks.at[5], kr.at[5], outer)
    kx_inner = remote(kx_half, kx_ri, ks.at[6], kr.at[6], inner)
    tx_inner = remote(tq.at[lo], tq.at[lo], ks.at[7], kr.at[7], inner)
    tx_outer = remote(turned, blk.at[s, pl.ds(2 * h, 2)], ks.at[8], kr.at[8], outer)
    tx_core = remote(blk.at[s], blk.at[s], ks.at[9], kr.at[9], core)

    def kept(w):
        return kx[pl.ds(pl.multiple_of((1 - s) * hv + h * nv, nv), nv), pl.ds(pl.multiple_of(w * hv, hv), hv)]

    def cross_send():
        kx_core.start()
        kx_core.wait()
        for p in range(4):
            w = slice((p % 2) * hv, (p % 2 + 1) * hv)
            k = kx[pl.ds(pl.multiple_of(s * hv + (p // 2) * nv, nv), nv), w] + kx_rc[tile(p // 2), w]
            kx_out[p] = k.astype(KSEND)
            kx[pl.ds(pl.multiple_of((1 - s) * hv + (p // 2) * nv, nv), nv), w] = k
        kx_outer.start()

    def cross_turn():
        kx_outer.wait()
        kx_half[...] = (kept(1 - lo) + kx_ro[1 - lo].astype(F32)).astype(KSEND)
        kx_inner.start()

    def cross_tiles():
        kx_inner.wait()
        m = kept(lo) + kx_ro[lo].astype(F32) + kx_ri[...].astype(F32)
        occ_k, occ_m = col, col + blocks
        for i in range(2):
            tq[lo, i] = amplitudes(m[:, i * nv:(i + 1) * nv], occ_m, 2 * s + h, occ_k, 2 * lo + i).astype(BF16)
        tx_inner.start()

    def cross_share():
        tx_inner.wait()
        for w in range(2):
            for i in range(2):
                t = tq[w, i]
                back = t.astype(F32).T.astype(BF16)
                blk[s, 2 * h + w, i] = jnp.where(h == 0, t, back)
                turned[w, i] = jnp.where(h == 0, back, t)
        tx_outer.start()

    def cross_swap():
        tx_outer.wait()
        tx_core.start()

    def cross_place():
        tx_core.wait()

        @pl.when(h == 0)
        def _():
            for ss in range(2):
                for xx in range(4):
                    for i in range(2):
                        tx[tile(2 * ss + xx // 2), tile(2 * (xx % 2) + i)] = blk[ss, xx, i]

        @pl.when(h == 1)
        def _():
            for ss in range(2):
                for xx in range(4):
                    for i in range(2):
                        tx[tile(2 * (xx % 2) + i), tile(2 * ss + xx // 2)] = blk[ss, xx, i]

    after = {}
    for step, todo in zip(STEPS, (diag_send, diag_tiles, pack, unpack, land, diag_place, cross_send, cross_turn,
                                  cross_tiles, cross_share, cross_swap, cross_place), strict=True):
        after.setdefault(step, []).append(todo)
    begin = 0
    for step in sorted(after):
        if step < CHUNKS:
            pl.loop(begin, step + 1)(met_step)
        else:
            if begin < CHUNKS:
                pl.loop(begin, CHUNKS)(met_step)
            for c in range(max(begin, CHUNKS), step + 1):
                far_wait(c - CHUNKS)
                if c + AHEAD < 2 * CHUNKS:
                    send(c + AHEAD)
        begin = step + 1
        for todo in after[step]:
            todo()
    ready = begin - CHUNKS

    def gamma(c, q, skip=0):
        g = jnp.dot(whole(own, last, q, at(c)), td[...], preferred_element_type=F32)
        g = g + jnp.dot(whole(far, far_last, q, at(c)), tx[...], preferred_element_type=F32)
        for i in range(slots):
            wide[q, pl.ds(i, size, stride=slots), :] = g[:, i * nv:(i + 1) * nv]
        at_row = slots * (q * start1 + c * size + skip)
        n = slots * (size - skip)
        out[pl.ds(pl.multiple_of(at_row, 64), n)] = wide[q, slots * skip:].astype(BF16)

    gamma(0, 0)
    gamma(0, 1, over)

    @pl.loop(1, ready)
    def _(c):
        for q in range(2):
            gamma(c, q)

    @pl.loop(ready, CHUNKS)
    def _(c):
        far_wait(c)

        @pl.when(c + AHEAD < CHUNKS)
        def _():
            for t in range(2):
                hop2(t, c + AHEAD).start()

        for q in range(2):
            gamma(c, q)

    @pl.loop(0, CHUNKS)
    def _(c):
        for q in range(2):
            hop1(q, c).wait_send()
            hop2(q, c).wait_send()


def half_rows(rows):
    unit = 16 * CHUNKS
    return -(-(rows // 2) // unit) * unit


def on_device(b_tensor, occ_energy, vir_energy, occ_count):
    rows, slots, nv = b_tensor.shape
    flat = slots * nv
    nh = half_rows(rows)
    size = nh // CHUNKS
    dims = (lax.axis_size("occ"), rows, nv, slots)
    smem, vmem, hbm = (pl.BlockSpec(memory_space=m) for m in (pltpu.SMEM, pltpu.VMEM, pl.ANY))
    half_up = slots * (slots + 1) // 4
    piece = -(-nh // (GROUP // 2) // 16) * 16

    def run(number, cap):
        return pl.pallas_call(
            functools.partial(kernel, dims, cap),
            out_shape=pltpu.VMEM((rows * slots, nv), BF16),
            in_specs=[smem, smem, vmem, hbm],
            out_specs=vmem,
            scratch_shapes=[
                pltpu.VMEM((2, CHUNKS, slots * size, nv), BF16),
                pltpu.VMEM((2, slots * size, nv), F32),
                pltpu.VMEM((2, nh, flat - nv), BF16),
                pltpu.VMEM((2, nh, nv), BF16),
                pltpu.VMEM((2, nh, flat - nv), BF16),
                pltpu.VMEM((2, nh, flat - nv), BF16),
                pltpu.VMEM((2, nh, nv), BF16),
                pltpu.VMEM((GROUP, piece, nv), BF16),
                pltpu.VMEM((cap, piece, nv), BF16),
                pltpu.VMEM((cap, piece, nv), BF16),
                pltpu.VMEM((GROUP, piece, nv), BF16),
                pltpu.VMEM((GROUP, piece, nv), BF16),
                pltpu.VMEM((flat, flat), F32),
                pltpu.VMEM((flat, flat), F32),
                pltpu.VMEM((half_up, nv, nv), F32),
                pltpu.VMEM((flat // 2, flat), F32),
                pltpu.VMEM((half_up, nv, nv), KSEND),
                pltpu.VMEM((half_up, nv, nv), KSEND),
                pltpu.VMEM((4, nv, flat // 2), KSEND),
                pltpu.VMEM((2, nv, flat // 2), KSEND),
                pltpu.VMEM((nv, flat // 2), KSEND),
                pltpu.VMEM((nv, flat // 2), KSEND),
                pltpu.VMEM((flat, flat), BF16),
                pltpu.VMEM((flat, flat), BF16),
                pltpu.VMEM((2, 2, nv, nv), BF16),
                pltpu.VMEM((2, 2, nv, nv), BF16),
                pltpu.VMEM((2, 4, 2, nv, nv), BF16),
                pltpu.VMEM((2, half_up, nv, nv), F32),
                pltpu.VMEM((2, half_up, nv, nv), BF16),
                pltpu.SemaphoreType.DMA((2, CHUNKS)),
                pltpu.SemaphoreType.DMA((2, CHUNKS)),
                pltpu.SemaphoreType.DMA((2, CHUNKS)),
                pltpu.SemaphoreType.DMA((2, CHUNKS)),
                pltpu.SemaphoreType.DMA((2, CHUNKS)),
                pltpu.SemaphoreType.DMA((12,)),
                pltpu.SemaphoreType.DMA((12,)),
                pltpu.SemaphoreType.DMA((2, GROUP)),
                pltpu.SemaphoreType.DMA((2, GROUP)),
            ],
            compiler_params=pltpu.CompilerParams(collective_id=number, has_side_effects=True,
                                                 vmem_limit_bytes=46 << 20),
        )(occ_energy, occ_count, vir_energy.reshape(1, nv), b_tensor.reshape(rows * slots, nv))

    full = (occ_count == slots).astype(jnp.int32).reshape(-1, GROUP).sum(axis=1)
    which = sum((full > cap).astype(jnp.int32) for cap in CAPS[:-1]).max()
    out = lax.switch(which, [functools.partial(run, n, cap) for n, cap in enumerate(CAPS)])
    return out.reshape(rows, slots, nv)


def solution(mesh):
    return jax.shard_map(
        on_device,
        mesh=mesh,
        in_specs=(P("aux", "occ", None), P(), P(), P()),
        out_specs=P("aux", "occ", None),
        check_vma=False,
    )
```
